32 devices in a mesh: tf: 4 (over y, x), gz: 4 (over z), sec: 2 (over core).
Axes of the slice: x: 2, y: 2, z: 4, core: 2. Of those that a mesh axis runs over, the one named last changes fastest.
Arguments:
- residuals: bfloat16 [3, 4, 4, 2, 4, 8192], P(None, 'tf', 'gz', 'sec'), may hold values from -6 to 6
- weights: bfloat16 [4, 4, 2, 4, 8192], P('tf', 'gz', 'sec'), may hold values from 0.5 to 2
- fraction: bfloat16 [4, 4, 2, 4, 8192], P('tf', 'gz', 'sec'), may hold values from 0 to 1
- voxels: int32 [3, 4, 4, 2, 4, 8192], P(None, 'tf', 'gz', 'sec'), may hold values from 0 to 255, as said below
- kernel_reach: int32 [152], P('sec'), may hold values from 1 to 4
Outputs:
- distortion: float32 [3, 256, 152, 180], P(None, ('tf', 'gz'), 'sec')
The draws below stay inside these ranges and needn't reach their ends.
Inputs may be any that keep to these rules, and one draw needn't show every extreme that they name: `voxels`: component 0 is the pad row, 1 the pad bin, 2 the drift bin. A residual at sec index s has its row in s * 76 to s * 76 + 75; its pad bin is at most 178; a residual at gz index g in slot t of the fifth dimension has its drift bin in block t * (number of gz devices) + g, that is among the 16 bins from (t * (number of gz devices) + g) * 16 on.
All inputs are finite; a program needn't handle non-finite values.
Results may differ from the reference program's by a relative error of at most 0.0026.
Values may be sent and summed in bfloat16 or wider, within the bound.
A program may use at most 64 MiB of HBM per device.

```python
import math
import jax
import jax.numpy as jnp
from jax import lax

ROWS = 152
PAD = 180
DRIFT = 256
RES_BLK = 8192
ROW_DEV = 76
DRIFT_DEV = 16
N_TF = 4
N_GZ = 4
N_SEC = 2


def draw_voxels(key, part):
    shape = (N_TF, N_GZ, N_SEC, N_TF, RES_BLK)
    first_key, second_key, third_key = jax.random.split(key, 3)
    gz_place = lax.broadcasted_iota(jnp.int32, shape, 1)
    sec_place = lax.broadcasted_iota(jnp.int32, shape, 2)
    target = lax.broadcasted_iota(jnp.int32, shape, 3)
    rows_at = sec_place * ROW_DEV + jax.random.randint(first_key, shape, 0, ROW_DEV)
    pads_at = jax.random.randint(second_key, shape, 0, PAD - 1)
    drift_at = (target * N_GZ + gz_place) * DRIFT_DEV + jax.random.randint(third_key, shape, 0, DRIFT_DEV)
    return jnp.stack([rows_at, pads_at, drift_at], 0).astype(jnp.int32)


def set_ends(array, own_key, low, top_value):
    spot = [jax.random.randint(jax.random.fold_in(own_key, axis), (), 0, length) for axis, length in enumerate(array.shape)]
    main_axis = array.shape.index(max(array.shape))
    neighbour = spot[:main_axis] + [(spot[main_axis] + 1) % array.shape[main_axis]] + spot[main_axis + 1:]
    return array.at[tuple(spot)].set(low).at[tuple(neighbour)].set(top_value)


def levels(key, dims, cuts, smallest, top_value):
    factor_of = 1.0
    for dim, blocks in cuts:
        steps = jax.random.uniform(jax.random.fold_in(jax.random.fold_in(key, 6), dim), (blocks,), jnp.float32, smallest / len(cuts), top_value / len(cuts))
        factor_of = factor_of * jnp.repeat(jnp.exp(steps), dims[dim] // blocks).reshape((-1,) + (1,) * (len(dims) - 1 - dim))
    return factor_of


def centred(rng, shape, deviation, bound, cuts=(), dtype=jnp.bfloat16):
    entries = jax.random.normal(rng, shape, jnp.float32) * deviation
    if len(cuts) > 0:
        entries = levels(rng, shape, cuts, -0.22, 0.18) * entries
    return jnp.clip(entries, min=-bound, max=bound).astype(dtype)


def setup_inputs(seed: int = 0) -> dict:
    key_of = jax.random.split(jax.random.key(seed), 6)
    return {
        "residuals": centred(key_of[0], (3, N_TF, N_GZ, N_SEC, N_TF, RES_BLK), 1.0, 6.0, ((1, 4), (2, 4), (3, 2))),
        "weights": jnp.clip(jnp.exp(math.log(2.0) - 1.3862944 * jax.random.uniform(key_of[1], (N_TF, N_GZ, N_SEC, N_TF, RES_BLK), jnp.float32) ** levels(key_of[1], (N_TF, N_GZ, N_SEC, N_TF, RES_BLK), ((0, 4), (1, 4), (2, 2)), -0.2, 0.2)), 0.5, 2.0).astype(jnp.bfloat16),
        "fraction": jnp.clip(1.0 * jax.random.uniform(key_of[2], (N_TF, N_GZ, N_SEC, N_TF, RES_BLK), jnp.float32) ** levels(key_of[2], (N_TF, N_GZ, N_SEC, N_TF, RES_BLK), ((0, 4), (1, 4), (2, 2)), -0.2, 0.2), 0.0, 1.0).astype(jnp.bfloat16),
        "voxels": draw_voxels(jax.random.fold_in(key_of[5], 71), 0),
        "kernel_reach": set_ends(jax.random.randint(key_of[4], (ROWS,), 1, 5), jax.random.fold_in(key_of[4], 1), 1, 4).astype(jnp.int32),
    }


def row_kernels(kernel_reach):
    spread = kernel_reach.astype(jnp.float32)[:, None, None]
    places = lax.broadcasted_iota(jnp.int32, (PAD, PAD), 0)
    others = lax.broadcasted_iota(jnp.int32, (PAD, PAD), 1)
    distance = jnp.abs(places - others).astype(jnp.float32)[None]
    return jnp.maximum(spread + 1.0 - distance, 0.0) / ((spread + 1.0) * (spread + 1.0))


def reference(residuals, weights, fraction, voxels, kernel_reach):
    components = residuals.reshape(3, -1).astype(jnp.float32)
    weight_all = weights.reshape(-1).astype(jnp.float32)
    share_all = fraction.reshape(-1).astype(jnp.float32)
    coords = voxels.reshape(3, -1)
    left_share = weight_all * (1.0 - share_all)
    right_share = weight_all * share_all
    left_chan = jnp.stack([left_share, left_share * components[0], left_share * components[1], left_share * components[2]], 1).astype(jnp.bfloat16)
    right_chan = jnp.stack([right_share, right_share * components[0], right_share * components[1], right_share * components[2]], 1).astype(jnp.bfloat16)
    left_chan, right_chan = lax.optimization_barrier((left_chan, right_chan))
    deposit = jnp.concatenate([left_chan.astype(jnp.float32), right_chan.astype(jnp.float32)], 0)
    flat = ((coords[2] * ROWS + coords[0]) * PAD + coords[1]).astype(jnp.int32)
    segment = jnp.concatenate([flat, flat + 1]).astype(jnp.int32)
    histogram = jax.ops.segment_sum(deposit, segment, num_segments=DRIFT * ROWS * PAD)
    histogram = histogram.reshape(DRIFT, ROWS, PAD, 4)
    means = histogram[..., 1:4] / (histogram[..., 0:1] + 1.0)
    means = jnp.transpose(means, (3, 0, 1, 2))
    across = jnp.einsum("kzrq,rpq->kzrp", means, row_kernels(kernel_reach), precision=lax.Precision.HIGHEST)
    padded = jnp.pad(across, ((0, 0), (0, 0), (2, 2), (0, 0)))
    smoothed = (padded[:, :, 0:ROWS] + 2.0 * padded[:, :, 1:ROWS + 1] + 3.0 * padded[:, :, 2:ROWS + 2]
                + 2.0 * padded[:, :, 3:ROWS + 3] + padded[:, :, 4:ROWS + 4]) / 9.0
    return jnp.cumsum(smoothed, axis=1)
```

```python
import functools

import jax
import jax.numpy as jnp
from jax import lax
from jax.experimental import pallas as pl
from jax.experimental.pallas import tpu as pltpu
from jax.sharding import PartitionSpec as P

PAD = 180
DRIFT = 256
PADS = 192
LANES = 256
TAPS = 5
MESH = pl.DeviceIdType.MESH
F32 = jnp.float32
BF16 = jnp.bfloat16


def round_up(value, unit):
    return (value + unit - 1) // unit * unit


def kernel(
    sizes,
    res_ref,
    weight_ref,
    frac_ref,
    vox_ref,
    reach_ref,
    out_ref,
    send_buf,
    recv_buf,
    hist,
    field,
    taps,
    low_out,
    high_out,
    low_in,
    high_in,
    last_out,
    last_in,
    totals,
    by_gz,
    by_tf,
    back,
    carry,
    res_send,
    res_recv,
    halo_send,
    halo_recv,
    scan_send,
    scan_recv,
):
    tf_count, gz_count, sec_count, drift_dev, row_dev, rows_pad, part, half, step = sizes
    my_tf = lax.axis_index("tf")
    my_gz = lax.axis_index("gz")
    my_sec = lax.axis_index("sec")
    has_low = my_sec > 0
    has_high = my_sec < sec_count - 1
    last = drift_dev - 1

    barrier = pltpu.get_barrier_semaphore()
    for s in range(1, tf_count):
        pl.semaphore_signal(
            barrier, inc=1, device_id={"tf": lax.rem(my_tf + s, tf_count)}, device_id_type=MESH
        )
    for s in range(1, gz_count):
        pl.semaphore_signal(
            barrier, inc=1, device_id={"gz": lax.rem(my_gz + s, gz_count)}, device_id_type=MESH
        )

    @pl.when(has_low)
    def _():
        pl.semaphore_signal(barrier, inc=1, device_id={"sec": my_sec - 1}, device_id_type=MESH)

    @pl.when(has_high)
    def _():
        pl.semaphore_signal(barrier, inc=1, device_id={"sec": my_sec + 1}, device_id_type=MESH)

    first_row = my_sec * row_dev
    channels = [res_ref[0], res_ref[1], res_ref[2], weight_ref[...], frac_ref[...]]
    channels = [c.astype(F32) for c in channels]
    channels.append((vox_ref[0] - first_row).astype(F32))
    channels.append(vox_ref[1].astype(F32))
    block_of = lax.broadcasted_iota(jnp.int32, vox_ref.shape[1:], 0)
    channels.append((vox_ref[2] - (block_of * gz_count + my_gz) * drift_dev).astype(F32))
    for t in range(tf_count):
        rows = [c[t : t + 1, h * half : (h + 1) * half] for h in range(2) for c in channels]
        send_buf[t] = jnp.concatenate(rows, axis=0).astype(BF16)

    neighbours = has_low.astype(jnp.int32) + has_high.astype(jnp.int32)
    pl.semaphore_wait(barrier, tf_count + gz_count - 2 + neighbours)

    def residual_copy(s):
        target = lax.rem(my_tf + s, tf_count)
        return pltpu.make_async_remote_copy(
            src_ref=send_buf.at[target],
            dst_ref=recv_buf.at[s],
            send_sem=res_send.at[s],
            recv_sem=res_recv.at[s],
            device_id={"tf": target},
            device_id_type=MESH,
        )

    for s in range(1, tf_count):
        residual_copy(s).start()
    recv_buf[0] = send_buf[my_tf]
    hist[...] = jnp.zeros_like(hist)

    reach = reach_ref[...].astype(F32)
    spread = jnp.broadcast_to(reach, (rows_pad, LANES)) + 1.0
    for d in range(TAPS):
        taps[d] = jnp.maximum(spread - float(d), 0.0) / (spread * spread * 9.0)

    steps = half // step
    width = 2 * step

    def deposit(number, _):
        s = number // steps
        j = number % steps

        @pl.when(jnp.logical_and(j == 0, s > 0))
        def _():
            residual_copy(s).wait_recv()

        block = recv_buf[s, :, pl.ds(pl.multiple_of(j * step, step), step)].astype(F32)
        data = jnp.concatenate([block[0:8], block[8:16]], axis=1)
        left = data[3:4] * (1.0 - data[4:5])
        right = data[3:4] * data[4:5]
        row_id = data[5:6].astype(BF16)
        pad_id = data[6:7].astype(BF16)
        next_id = (data[6:7] + 1.0).astype(BF16)
        drift_id = data[7:8]
        pad_iota = lax.broadcasted_iota(jnp.int32, (PADS, width), 0).astype(BF16)
        row_iota = lax.broadcasted_iota(jnp.int32, (rows_pad, width), 0).astype(BF16)
        at_left = pad_iota == pad_id
        at_right = pad_iota == next_id
        nothing = jnp.zeros((PADS, width), BF16)
        parts = []
        for c in range(4):
            l_val = left if c == 0 else left * data[c - 1 : c]
            r_val = right if c == 0 else right * data[c - 1 : c]
            l_all = jnp.broadcast_to(l_val.astype(BF16), (PADS, width))
            r_all = jnp.broadcast_to(r_val.astype(BF16), (PADS, width))
            parts.append(jnp.where(at_left, l_all, jnp.where(at_right, r_all, nothing)))
        columns = jnp.concatenate(parts, axis=0)
        at_row = jnp.where(
            row_iota == row_id,
            jnp.ones((rows_pad, width), BF16),
            jnp.zeros((rows_pad, width), BF16),
        )
        cells = []
        for z in range(drift_dev):
            chosen = jnp.where(drift_id == float(z), 1.0, 0.0).astype(BF16)
            cells.append(at_row * chosen)
        cells = jnp.concatenate(cells, axis=0)
        hist[...] += lax.dot_general(
            cells, columns, (((1,), (1,)), ((), ())), preferred_element_type=F32
        )
        return 0

    lax.fori_loop(0, tf_count * steps, deposit, 0)

    lane = lax.broadcasted_iota(jnp.int32, (rows_pad, LANES), 1)
    inside = lane < PAD
    field[:, last] = jnp.zeros((3, rows_pad, LANES), F32)

    def channel(z, c):
        start = c * PADS // 128 * 128
        rows = pl.ds(pl.multiple_of(z * rows_pad, rows_pad), rows_pad)
        piece = hist[rows, start : start + LANES]
        if c * PADS != start:
            piece = pltpu.roll(piece, LANES - (c * PADS - start), 1)
        return piece

    def average(z, _):
        before = jnp.where(z == 0, last, z - 1)
        scale = 1.0 / (channel(z, 0) + 1.0)
        for k in range(3):
            mean = jnp.where(inside, channel(z, k + 1) * scale, 0.0)
            field[k, z] = field[k, before] + mean
        return 0

    lax.fori_loop(0, drift_dev, average, 0)

    def across(k, z):
        x = field[k, z]
        total = taps[0] * x
        for d in range(1, TAPS):
            total += taps[d] * (pltpu.roll(x, d, 1) + pltpu.roll(x, LANES - d, 1))
        field[k, z] = total

    def down(k, z):
        x = field[k, z]
        near = pltpu.roll(x, 1, 0) + pltpu.roll(x, rows_pad - 1, 0)
        far = pltpu.roll(x, 2, 0) + pltpu.roll(x, rows_pad - 2, 0)
        return 3.0 * x + 2.0 * near + far

    def to_low(src, dst, i):
        return pltpu.make_async_remote_copy(
            src_ref=src, dst_ref=dst, send_sem=halo_send.at[i], recv_sem=halo_recv.at[i],
            device_id={"sec": my_sec - 1}, device_id_type=MESH,
        )

    def to_high(src, dst, i):
        return pltpu.make_async_remote_copy(
            src_ref=src, dst_ref=dst, send_sem=halo_send.at[i], recv_sem=halo_recv.at[i],
            device_id={"sec": my_sec + 1}, device_id_type=MESH,
        )

    last_out[...] = jnp.zeros_like(last_out)
    for k in range(3):
        across(k, last)
        for j in range(2):
            last_out[0, pl.ds(k * 2 + j, 1)] = field[k, last, pl.ds(j, 1)]
            last_out[1, pl.ds(k * 2 + j, 1)] = field[k, last, pl.ds(row_dev - 2 + j, 1)]
    last_low = to_low(last_out.at[0], last_in.at[1], 0)
    last_high = to_high(last_out.at[1], last_in.at[0], 1)
    both_low = to_low(low_out, high_in, 2)
    both_high = to_high(high_out, low_in, 3)

    @pl.when(has_low)
    def _():
        last_low.start()

    @pl.when(has_high)
    def _():
        last_high.start()

    def widen(z, _):
        for k in range(3):
            across(k, z)
            for j in range(2):
                low_out[j, k, pl.ds(z, 1)] = field[k, z, pl.ds(j, 1)]
                high_out[j, k, pl.ds(z, 1)] = field[k, z, pl.ds(row_dev - 2 + j, 1)]
        return 0

    @pl.when(has_high)
    def _():
        last_low.wait_recv()
        for k in range(3):
            field[k, last, pl.ds(row_dev, 2)] = last_in[1, pl.ds(k * 2, 2)]

    @pl.when(has_low)
    def _():
        last_high.wait_recv()
        for k in range(3):
            field[k, last, pl.ds(rows_pad - 2, 2)] = last_in[0, pl.ds(k * 2, 2)]

    totals[...] = jnp.zeros_like(totals)
    for k in range(3):
        totals[pl.ds(k * rows_pad, rows_pad)] = down(k, last)

    def first_copy(s):
        target = lax.rem(my_gz + s, gz_count)
        return pltpu.make_async_remote_copy(
            src_ref=totals.at[pl.ds(pl.multiple_of(target * part, part), part)],
            dst_ref=by_gz.at[my_gz],
            send_sem=scan_send.at[0, s], recv_sem=scan_recv.at[0, s],
            device_id={"gz": target}, device_id_type=MESH,
        )

    def second_copy(s):
        target = lax.rem(my_tf + s, tf_count)
        return pltpu.make_async_remote_copy(
            src_ref=by_tf.at[my_tf], dst_ref=by_tf.at[my_tf],
            send_sem=scan_send.at[1, s], recv_sem=scan_recv.at[1, s],
            device_id={"tf": target}, device_id_type=MESH,
        )

    def third_copy(s):
        target = lax.rem(my_gz + s, gz_count)
        return pltpu.make_async_remote_copy(
            src_ref=back.at[target],
            dst_ref=carry.at[pl.ds(pl.multiple_of(my_gz * part, part), part)],
            send_sem=scan_send.at[2, s], recv_sem=scan_recv.at[2, s],
            device_id={"gz": target}, device_id_type=MESH,
        )

    for s in range(1, gz_count):
        first_copy(s).start()
    by_gz[my_gz] = totals[pl.ds(pl.multiple_of(my_gz * part, part), part)]

    lax.fori_loop(0, last, widen, 0)

    @pl.when(has_low)
    def _():
        both_low.start()

    @pl.when(has_high)
    def _():
        both_high.start()

    for s in range(1, gz_count):
        first_copy(s).wait_recv()
    column = by_gz[0]
    for g in range(1, gz_count):
        column += by_gz[g]
    by_tf[my_tf] = column
    for s in range(1, tf_count):
        second_copy(s).start()

    @pl.when(has_high)
    def _():
        both_low.wait_recv()

    @pl.when(has_low)
    def _():
        both_high.wait_recv()

    def fill(z, _):
        @pl.when(has_high)
        def _():
            for k in range(3):
                for j in range(2):
                    field[k, z, pl.ds(row_dev + j, 1)] = high_in[j, k, pl.ds(z, 1)]

        @pl.when(has_low)
        def _():
            for k in range(3):
                for j in range(2):
                    field[k, z, pl.ds(rows_pad - 2 + j, 1)] = low_in[j, k, pl.ds(z, 1)]

        return 0

    lax.fori_loop(0, last, fill, 0)

    for s in range(1, tf_count):
        second_copy(s).wait_recv()
    base = jnp.zeros((part, LANES), F32)
    for t in range(tf_count):
        base += jnp.where(t < my_tf, by_tf[t], 0.0)
    for g in range(gz_count):
        back[g] = base
        base = base + by_gz[g]
    for s in range(1, gz_count):
        third_copy(s).start()
    carry[pl.ds(pl.multiple_of(my_gz * part, part), part)] = back[my_gz]

    def narrow(z, _):
        for k in range(3):
            field[k, z] = down(k, z)
        return 0

    lax.fori_loop(0, last, narrow, 0)
    for k in range(3):
        field[k, last] = totals[pl.ds(k * rows_pad, rows_pad)]

    for s in range(1, gz_count):
        third_copy(s).wait_recv()

    def finish(z, _):
        for k in range(3):
            whole = field[k, z] + carry[pl.ds(k * rows_pad, rows_pad)]
            out_ref[k, z] = whole[:row_dev, :PAD]
        return 0

    lax.fori_loop(0, drift_dev, finish, 0)

    for s in range(1, tf_count):
        residual_copy(s).wait_send()
        second_copy(s).wait_send()
    for s in range(1, gz_count):
        first_copy(s).wait_send()
        third_copy(s).wait_send()

    @pl.when(has_low)
    def _():
        last_low.wait_send()
        both_low.wait_send()

    @pl.when(has_high)
    def _():
        last_high.wait_send()
        both_high.wait_send()


def per_device(residuals, weights, fraction, voxels, kernel_reach):
    tf_count = lax.axis_size("tf")
    gz_count = lax.axis_size("gz")
    sec_count = lax.axis_size("sec")
    drift_dev = DRIFT // (tf_count * gz_count)
    row_dev = kernel_reach.shape[0]
    rows_pad = round_up(row_dev + 4, 16)
    part = round_up(-(-3 * rows_pad // gz_count), 8)
    slots = weights.shape[-1]
    half = slots // 2
    step = min(512, half)
    sizes = (tf_count, gz_count, sec_count, drift_dev, row_dev, rows_pad, part, half, step)
    reach = jnp.pad(kernel_reach, (0, rows_pad - row_dev), constant_values=1)[:, None]
    vmem = pl.BlockSpec(memory_space=pltpu.VMEM)
    bins = round_up(drift_dev, 8)
    return pl.pallas_call(
        functools.partial(kernel, sizes),
        out_shape=jax.ShapeDtypeStruct((3, drift_dev, row_dev, PAD), F32),
        in_specs=[vmem] * 5,
        out_specs=vmem,
        scratch_shapes=[
            pltpu.VMEM((tf_count, 16, half), BF16),
            pltpu.VMEM((tf_count, 16, half), BF16),
            pltpu.VMEM((drift_dev * rows_pad, 4 * PADS), F32),
            pltpu.VMEM((3, drift_dev, rows_pad, LANES), F32),
            pltpu.VMEM((TAPS, rows_pad, LANES), F32),
            pltpu.VMEM((2, 3, bins, LANES), F32),
            pltpu.VMEM((2, 3, bins, LANES), F32),
            pltpu.VMEM((2, 3, bins, LANES), F32),
            pltpu.VMEM((2, 3, bins, LANES), F32),
            pltpu.VMEM((2, 8, LANES), F32),
            pltpu.VMEM((2, 8, LANES), F32),
            pltpu.VMEM((gz_count * part, LANES), F32),
            pltpu.VMEM((gz_count, part, LANES), F32),
            pltpu.VMEM((tf_count, part, LANES), F32),
            pltpu.VMEM((gz_count, part, LANES), F32),
            pltpu.VMEM((gz_count * part, LANES), F32),
            pltpu.SemaphoreType.DMA((tf_count,)),
            pltpu.SemaphoreType.DMA((tf_count,)),
            pltpu.SemaphoreType.DMA((4,)),
            pltpu.SemaphoreType.DMA((4,)),
            pltpu.SemaphoreType.DMA((3, max(tf_count, gz_count))),
            pltpu.SemaphoreType.DMA((3, max(tf_count, gz_count))),
        ],
        compiler_params=pltpu.CompilerParams(
            collective_id=0, has_side_effects=True, vmem_limit_bytes=56 * 1024 * 1024
        ),
    )(
        residuals[:, 0, 0, 0],
        weights[0, 0, 0],
        fraction[0, 0, 0],
        voxels[:, 0, 0, 0],
        reach,
    )


def solution(mesh):
    placed = (
        P(None, "tf", "gz", "sec", None, None),
        P("tf", "gz", "sec", None, None),
        P("tf", "gz", "sec", None, None),
        P(None, "tf", "gz", "sec", None, None),
        P("sec"),
    )
    return jax.shard_map(
        per_device,
        mesh=mesh,
        in_specs=placed,
        out_specs=P(None, ("tf", "gz"), "sec", None),
        check_vma=False,
    )
```

```python
import functools

import jax
import jax.numpy as jnp
from jax import lax
from jax.experimental import pallas as pl
from jax.experimental.pallas import tpu as pltpu
from jax.sharding import PartitionSpec as P

PAD = 180
DRIFT = 256
PADS = 192
LANES = 256
TAPS = 5
MESH = pl.DeviceIdType.MESH
F32 = jnp.float32
BF16 = jnp.bfloat16


def round_up(value, unit):
    return (value + unit - 1) // unit * unit


def kernel(
    sizes,
    res_ref,
    weight_ref,
    frac_ref,
    vox_ref,
    reach_ref,
    out_ref,
    send_buf,
    recv_buf,
    cells_even,
    cells_odd,
    columns_even,
    columns_odd,
    hist,
    field,
    sums,
    taps,
    last_out,
    last_in,
    totals,
    by_gz,
    by_tf,
    back,
    carry,
    res_send,
    res_recv,
    halo_send,
    halo_recv,
    scan_send,
    scan_recv,
):
    tf_count, gz_count, sec_count, drift_dev, drift_pad, row_dev, rows_pad, part, half, step = sizes
    my_tf = lax.axis_index("tf")
    my_gz = lax.axis_index("gz")
    my_sec = lax.axis_index("sec")
    has_low = my_sec > 0
    has_high = my_sec < sec_count - 1
    group = 4 if row_dev % 4 == 0 else 1

    for r in (0, 1, row_dev + 2, row_dev + 3):
        field[:, r] = jnp.zeros((3, drift_pad, LANES), F32)

    barrier = pltpu.get_barrier_semaphore()
    for s in range(1, tf_count):
        pl.semaphore_signal(
            barrier, inc=1, device_id={"tf": lax.rem(my_tf + s, tf_count)}, device_id_type=MESH
        )
    for s in range(1, gz_count):
        pl.semaphore_signal(
            barrier, inc=1, device_id={"gz": lax.rem(my_gz + s, gz_count)}, device_id_type=MESH
        )

    @pl.when(has_low)
    def _():
        pl.semaphore_signal(barrier, inc=1, device_id={"sec": my_sec - 1}, device_id_type=MESH)

    @pl.when(has_high)
    def _():
        pl.semaphore_signal(barrier, inc=1, device_id={"sec": my_sec + 1}, device_id_type=MESH)

    first_row = my_sec * row_dev
    channels = [res_ref[0], res_ref[1], res_ref[2], weight_ref[...], frac_ref[...]]
    channels = [c.astype(F32) for c in channels]
    channels.append((vox_ref[0] - first_row).astype(F32))
    channels.append(vox_ref[1].astype(F32))
    block_of = lax.broadcasted_iota(jnp.int32, vox_ref.shape[1:], 0)
    channels.append((vox_ref[2] - (block_of * gz_count + my_gz) * drift_dev).astype(F32))
    for t in range(tf_count):
        rows = [c[t : t + 1, h * half : (h + 1) * half] for h in range(2) for c in channels]
        send_buf[t] = jnp.concatenate(rows, axis=0).astype(BF16)

    neighbours = has_low.astype(jnp.int32) + has_high.astype(jnp.int32)
    pl.semaphore_wait(barrier, tf_count + gz_count - 2 + neighbours)

    def residual_copy(s):
        target = lax.rem(my_tf + s, tf_count)
        return pltpu.make_async_remote_copy(
            src_ref=send_buf.at[target],
            dst_ref=recv_buf.at[s],
            send_sem=res_send.at[s],
            recv_sem=res_recv.at[s],
            device_id={"tf": target},
            device_id_type=MESH,
        )

    for s in range(1, tf_count):
        residual_copy(s).start()
    recv_buf[0] = send_buf[my_tf]
    hist[...] = jnp.zeros_like(hist)

    reach = reach_ref[...].astype(F32)
    spread = jnp.broadcast_to(reach, (rows_pad, LANES)) + 1.0
    for d in range(TAPS):
        taps[d] = jnp.maximum(spread - float(d), 0.0) / (spread * spread * 9.0)

    steps = half // step
    width = 2 * step

    total = tf_count * steps

    def spread_out(number, cells, columns):
        s = number // steps
        j = number % steps
        block = recv_buf[s, :, pl.ds(pl.multiple_of(j * step, step), step)].astype(F32)
        data = jnp.concatenate([block[0:8], block[8:16]], axis=1)
        left = data[3:4] * (1.0 - data[4:5])
        right = data[3:4] * data[4:5]
        pad_id = data[6:7].astype(BF16)
        next_id = (data[6:7] + 1.0).astype(BF16)
        pad_iota = lax.broadcasted_iota(jnp.int32, (PADS, width), 0).astype(BF16)
        at_left = pad_iota == pad_id
        at_right = pad_iota == next_id
        nothing = jnp.zeros((PADS, width), BF16)
        for c in range(4):
            l_val = left if c == 0 else left * data[c - 1 : c]
            r_val = right if c == 0 else right * data[c - 1 : c]
            l_all = jnp.broadcast_to(l_val.astype(BF16), (PADS, width))
            r_all = jnp.broadcast_to(r_val.astype(BF16), (PADS, width))
            columns[c * PADS : (c + 1) * PADS] = jnp.where(
                at_left, l_all, jnp.where(at_right, r_all, nothing)
            )
        tile = (drift_pad, width)
        drift_iota = lax.broadcasted_iota(jnp.int32, tile, 0).astype(BF16)
        at_drift = jnp.where(
            drift_iota == data[7:8].astype(BF16), jnp.ones(tile, BF16), jnp.zeros(tile, BF16)
        )
        row_id = jnp.broadcast_to(data[5:6].astype(BF16), tile)
        for r in range(row_dev):
            cells[r * drift_pad : (r + 1) * drift_pad] = jnp.where(
                row_id == jnp.full(tile, r, BF16), at_drift, jnp.zeros(tile, BF16)
            )

    def add_up(cells, columns):
        hist[...] += lax.dot_general(
            cells[...], columns[...], (((1,), (1,)), ((), ())), preferred_element_type=F32
        )

    spread_out(0, cells_even, columns_even)

    def deposit(pair, _):
        later = 2 * pair + 2

        @pl.when(jnp.logical_and(later % steps == 0, later < total))
        def _():
            residual_copy(later // steps).wait_recv()

        add_up(cells_even, columns_even)
        spread_out(2 * pair + 1, cells_odd, columns_odd)
        add_up(cells_odd, columns_odd)
        spread_out(jnp.minimum(later, total - 1), cells_even, columns_even)
        return 0

    lax.fori_loop(0, total // 2, deposit, 0)

    inside = lax.broadcasted_iota(jnp.int32, (drift_pad, LANES), 1) < PAD
    sums[...] = jnp.zeros_like(sums)

    def channel(r, c):
        start = c * PADS // 128 * 128
        rows = pl.ds(pl.multiple_of(r * drift_pad, drift_pad), drift_pad)
        piece = hist[rows, start : start + LANES]
        if c * PADS != start:
            piece = pltpu.roll(piece, LANES - (c * PADS - start), 1)
        return piece

    def each_row(work):
        def some(number, _):
            for i in range(group):
                work(number * group + i)
            return 0

        lax.fori_loop(0, row_dev // group, some, 0)

    def average(r):
        scale = 1.0 / (channel(r, 0) + 1.0)
        for k in range(3):
            mean = jnp.where(inside, channel(r, k + 1) * scale, 0.0)
            field[k, r + 2] = mean
            sums[k, pl.ds(r, 1)] = jnp.sum(mean, axis=0, keepdims=True)

    each_row(average)

    def across(x, weight):
        total = weight[0] * x
        for d in range(1, TAPS):
            total += weight[d] * (pltpu.roll(x, d, 1) + pltpu.roll(x, LANES - d, 1))
        return total

    def down(x):
        near = pltpu.roll(x, 1, 0) + pltpu.roll(x, rows_pad - 1, 0)
        far = pltpu.roll(x, 2, 0) + pltpu.roll(x, rows_pad - 2, 0)
        return 3.0 * x + 2.0 * near + far

    def to_low(src, dst, i):
        return pltpu.make_async_remote_copy(
            src_ref=src, dst_ref=dst, send_sem=halo_send.at[i], recv_sem=halo_recv.at[i],
            device_id={"sec": my_sec - 1}, device_id_type=MESH,
        )

    def to_high(src, dst, i):
        return pltpu.make_async_remote_copy(
            src_ref=src, dst_ref=dst, send_sem=halo_send.at[i], recv_sem=halo_recv.at[i],
            device_id={"sec": my_sec + 1}, device_id_type=MESH,
        )

    last_out[...] = jnp.zeros_like(last_out)
    for k in range(3):
        sums[k] = across(sums[k], taps)
        for j in range(2):
            last_out[0, pl.ds(k * 2 + j, 1)] = sums[k, pl.ds(j, 1)]
            last_out[1, pl.ds(k * 2 + j, 1)] = sums[k, pl.ds(row_dev - 2 + j, 1)]
    last_low = to_low(last_out.at[0], last_in.at[1], 0)
    last_high = to_high(last_out.at[1], last_in.at[0], 1)
    both_low = to_low(field.at[:, pl.ds(2, 2)], field.at[:, pl.ds(row_dev + 2, 2)], 2)
    both_high = to_high(field.at[:, pl.ds(row_dev, 2)], field.at[:, pl.ds(0, 2)], 3)

    @pl.when(has_low)
    def _():
        last_low.start()

    @pl.when(has_high)
    def _():
        last_high.start()

    @pl.when(has_high)
    def _():
        last_low.wait_recv()
        for k in range(3):
            sums[k, pl.ds(row_dev, 2)] = last_in[1, pl.ds(k * 2, 2)]

    @pl.when(has_low)
    def _():
        last_high.wait_recv()
        for k in range(3):
            sums[k, pl.ds(rows_pad - 2, 2)] = last_in[0, pl.ds(k * 2, 2)]

    totals[...] = jnp.zeros_like(totals)
    for k in range(3):
        totals[pl.ds(k * rows_pad, rows_pad)] = down(sums[k])

    def first_copy(s):
        target = lax.rem(my_gz + s, gz_count)
        return pltpu.make_async_remote_copy(
            src_ref=totals.at[pl.ds(pl.multiple_of(target * part, part), part)],
            dst_ref=by_gz.at[my_gz],
            send_sem=scan_send.at[0, s], recv_sem=scan_recv.at[0, s],
            device_id={"gz": target}, device_id_type=MESH,
        )

    def second_copy(s):
        target = lax.rem(my_tf + s, tf_count)
        return pltpu.make_async_remote_copy(
            src_ref=by_tf.at[my_tf], dst_ref=by_tf.at[my_tf],
            send_sem=scan_send.at[1, s], recv_sem=scan_recv.at[1, s],
            device_id={"tf": target}, device_id_type=MESH,
        )

    def third_copy(s):
        target = lax.rem(my_gz + s, gz_count)
        return pltpu.make_async_remote_copy(
            src_ref=back.at[target],
            dst_ref=carry.at[pl.ds(pl.multiple_of(my_gz * part, part), part)],
            send_sem=scan_send.at[2, s], recv_sem=scan_recv.at[2, s],
            device_id={"gz": target}, device_id_type=MESH,
        )

    for s in range(1, gz_count):
        first_copy(s).start()
    by_gz[my_gz] = totals[pl.ds(pl.multiple_of(my_gz * part, part), part)]

    drift_iota = lax.broadcasted_iota(jnp.int32, (drift_pad, LANES), 0)

    def widen(r):
        weight = [
            jnp.broadcast_to(taps[d, pl.ds(r, 1)], (drift_pad, LANES)) for d in range(TAPS)
        ]
        for k in range(3):
            x = across(field[k, r + 2], weight)
            d = 1
            while d < drift_dev:
                x += jnp.where(drift_iota >= d, pltpu.roll(x, d, 0), 0.0)
                d *= 2
            field[k, r + 2] = x

    each_row(widen)

    @pl.when(has_low)
    def _():
        both_low.start()

    @pl.when(has_high)
    def _():
        both_high.start()

    for s in range(1, gz_count):
        first_copy(s).wait_recv()
    column = by_gz[0]
    for g in range(1, gz_count):
        column += by_gz[g]
    by_tf[my_tf] = column
    for s in range(1, tf_count):
        second_copy(s).start()

    for s in range(1, tf_count):
        second_copy(s).wait_recv()
    base = jnp.zeros((part, LANES), F32)
    for t in range(tf_count):
        base += jnp.where(t < my_tf, by_tf[t], 0.0)
    for g in range(gz_count):
        back[g] = base
        base = base + by_gz[g]
    for s in range(1, gz_count):
        third_copy(s).start()
    carry[pl.ds(pl.multiple_of(my_gz * part, part), part)] = back[my_gz]

    @pl.when(has_high)
    def _():
        both_low.wait_recv()

    @pl.when(has_low)
    def _():
        both_high.wait_recv()

    for s in range(1, gz_count):
        third_copy(s).wait_recv()

    def finish(r):
        for k in range(3):
            near = field[k, r + 1] + field[k, r + 3]
            far = field[k, r] + field[k, r + 4]
            before = carry[pl.ds(k * rows_pad + r, 1)]
            whole = 3.0 * field[k, r + 2] + 2.0 * near + far + before
            out_ref[k, r] = whole[:drift_dev, :PAD]

    each_row(finish)

    for s in range(1, tf_count):
        residual_copy(s).wait_send()
        second_copy(s).wait_send()
    for s in range(1, gz_count):
        first_copy(s).wait_send()
        third_copy(s).wait_send()

    @pl.when(has_low)
    def _():
        last_low.wait_send()
        both_low.wait_send()

    @pl.when(has_high)
    def _():
        last_high.wait_send()
        both_high.wait_send()


def per_device(residuals, weights, fraction, voxels, kernel_reach):
    tf_count = lax.axis_size("tf")
    gz_count = lax.axis_size("gz")
    sec_count = lax.axis_size("sec")
    drift_dev = DRIFT // (tf_count * gz_count)
    drift_pad = round_up(drift_dev, 16)
    row_dev = kernel_reach.shape[0]
    rows_pad = round_up(row_dev + 4, 16)
    part = round_up(-(-3 * rows_pad // gz_count), 8)
    slots = weights.shape[-1]
    half = slots // 2
    step = min(512, half)
    sizes = (
        tf_count, gz_count, sec_count, drift_dev, drift_pad, row_dev, rows_pad, part, half, step
    )
    reach = jnp.pad(kernel_reach, (0, rows_pad - row_dev), constant_values=1)[:, None]
    vmem = pl.BlockSpec(memory_space=pltpu.VMEM)
    maps = pl.pallas_call(
        functools.partial(kernel, sizes),
        out_shape=jax.ShapeDtypeStruct((3, row_dev, drift_dev, PAD), F32),
        in_specs=[vmem] * 5,
        out_specs=vmem,
        scratch_shapes=[
            pltpu.VMEM((tf_count, 16, half), BF16),
            pltpu.VMEM((tf_count, 16, half), BF16),
            pltpu.VMEM((row_dev * drift_pad, 2 * step), BF16),
            pltpu.VMEM((row_dev * drift_pad, 2 * step), BF16),
            pltpu.VMEM((4 * PADS, 2 * step), BF16),
            pltpu.VMEM((4 * PADS, 2 * step), BF16),
            pltpu.VMEM((row_dev * drift_pad, 4 * PADS), F32),
            pltpu.VMEM((3, row_dev + 4, drift_pad, LANES), F32),
            pltpu.VMEM((3, rows_pad, LANES), F32),
            pltpu.VMEM((TAPS, rows_pad, LANES), F32),
            pltpu.VMEM((2, 8, LANES), F32),
            pltpu.VMEM((2, 8, LANES), F32),
            pltpu.VMEM((gz_count * part, LANES), F32),
            pltpu.VMEM((gz_count, part, LANES), F32),
            pltpu.VMEM((tf_count, part, LANES), F32),
            pltpu.VMEM((gz_count, part, LANES), F32),
            pltpu.VMEM((gz_count * part, LANES), F32),
            pltpu.SemaphoreType.DMA((tf_count,)),
            pltpu.SemaphoreType.DMA((tf_count,)),
            pltpu.SemaphoreType.DMA((4,)),
            pltpu.SemaphoreType.DMA((4,)),
            pltpu.SemaphoreType.DMA((3, max(tf_count, gz_count))),
            pltpu.SemaphoreType.DMA((3, max(tf_count, gz_count))),
        ],
        compiler_params=pltpu.CompilerParams(
            collective_id=0, has_side_effects=True, vmem_limit_bytes=56 * 1024 * 1024
        ),
    )(
        residuals[:, 0, 0, 0],
        weights[0, 0, 0],
        fraction[0, 0, 0],
        voxels[:, 0, 0, 0],
        reach,
    )
    return jnp.transpose(maps, (0, 2, 1, 3))


def solution(mesh):
    placed = (
        P(None, "tf", "gz", "sec", None, None),
        P("tf", "gz", "sec", None, None),
        P("tf", "gz", "sec", None, None),
        P(None, "tf", "gz", "sec", None, None),
        P("sec"),
    )
    return jax.shard_map(
        per_device,
        mesh=mesh,
        in_specs=placed,
        out_specs=P(None, ("tf", "gz"), "sec", None),
        check_vma=False,
    )
```

```python
import functools

import jax
import jax.numpy as jnp
from jax import lax
from jax.experimental import pallas as pl
from jax.experimental.pallas import tpu as pltpu
from jax.sharding import PartitionSpec as P

PAD = 180
DRIFT = 256
PADS = 192
LANES = 256
TAPS = 5
MESH = pl.DeviceIdType.MESH
F32 = jnp.float32
BF16 = jnp.bfloat16


def round_up(value, unit):
    return (value + unit - 1) // unit * unit


def kernel(
    sizes,
    res_ref,
    weight_ref,
    frac_ref,
    vox_ref,
    reach_ref,
    out_ref,
    carry,
    send_buf,
    recv_buf,
    cells_even,
    cells_odd,
    columns_even,
    columns_odd,
    hist,
    field,
    sums,
    taps,
    last_out,
    last_in,
    totals,
    by_gz,
    by_tf,
    back,
    local,
    res_send,
    res_recv,
    halo_send,
    halo_recv,
    scan_send,
    scan_recv,
    out_sem,
):
    tf_count, gz_count, sec_count, drift_dev, drift_pad, row_dev, rows_pad, part, half, step = sizes
    my_tf = lax.axis_index("tf")
    my_gz = lax.axis_index("gz")
    my_sec = lax.axis_index("sec")
    has_low = my_sec > 0
    has_high = my_sec < sec_count - 1

    for r in (0, 1, row_dev + 2, row_dev + 3):
        field[:, r] = jnp.zeros((3, drift_pad, LANES), F32)

    barrier = pltpu.get_barrier_semaphore()
    for s in range(1, tf_count):
        pl.semaphore_signal(
            barrier, inc=1, device_id={"tf": lax.rem(my_tf + s, tf_count)}, device_id_type=MESH
        )
    for s in range(1, gz_count):
        pl.semaphore_signal(
            barrier, inc=1, device_id={"gz": lax.rem(my_gz + s, gz_count)}, device_id_type=MESH
        )

    @pl.when(has_low)
    def _():
        pl.semaphore_signal(barrier, inc=1, device_id={"sec": my_sec - 1}, device_id_type=MESH)

    @pl.when(has_high)
    def _():
        pl.semaphore_signal(barrier, inc=1, device_id={"sec": my_sec + 1}, device_id_type=MESH)

    first_row = my_sec * row_dev
    channels = [res_ref[0], res_ref[1], res_ref[2], weight_ref[...], frac_ref[...]]
    channels = [c.astype(F32) for c in channels]
    channels.append((vox_ref[0] - first_row).astype(F32))
    channels.append(vox_ref[1].astype(F32))
    block_of = lax.broadcasted_iota(jnp.int32, vox_ref.shape[1:], 0)
    channels.append((vox_ref[2] - (block_of * gz_count + my_gz) * drift_dev).astype(F32))
    for t in range(tf_count):
        rows = [c[t : t + 1, h * half : (h + 1) * half] for h in range(2) for c in channels]
        send_buf[t] = jnp.concatenate(rows, axis=0).astype(BF16)

    neighbours = has_low.astype(jnp.int32) + has_high.astype(jnp.int32)
    pl.semaphore_wait(barrier, tf_count + gz_count - 2 + neighbours)

    def residual_copy(s):
        target = lax.rem(my_tf + s, tf_count)
        return pltpu.make_async_remote_copy(
            src_ref=send_buf.at[target],
            dst_ref=recv_buf.at[s],
            send_sem=res_send.at[s],
            recv_sem=res_recv.at[s],
            device_id={"tf": target},
            device_id_type=MESH,
        )

    for s in range(1, tf_count):
        residual_copy(s).start()
    recv_buf[0] = send_buf[my_tf]
    hist[...] = jnp.zeros_like(hist)

    square = (rows_pad, row_dev)
    diagonal = lax.broadcasted_iota(jnp.int32, square, 0) == lax.broadcasted_iota(
        jnp.int32, square, 1
    )
    reach = jnp.broadcast_to(reach_ref[...].astype(F32), square)
    reach = jnp.sum(jnp.where(diagonal, reach, 0.0), axis=1, keepdims=True)
    spread = jnp.broadcast_to(reach, (rows_pad, LANES)) + 1.0
    for d in range(TAPS):
        taps[d] = jnp.maximum(spread - float(d), 0.0) / (spread * spread * 9.0)

    steps = half // step
    width = 2 * step

    total = tf_count * steps

    def spread_out(number, cells, columns):
        s = number // steps
        j = number % steps
        block = recv_buf[s, :, pl.ds(pl.multiple_of(j * step, step), step)].astype(F32)
        data = jnp.concatenate([block[0:8], block[8:16]], axis=1)
        left = data[3:4] * (1.0 - data[4:5])
        right = data[3:4] * data[4:5]
        pad_id = data[6:7].astype(BF16)
        next_id = (data[6:7] + 1.0).astype(BF16)
        pad_iota = lax.broadcasted_iota(jnp.int32, (PADS, width), 0).astype(BF16)
        at_left = pad_iota == pad_id
        at_right = pad_iota == next_id
        nothing = jnp.zeros((PADS, width), BF16)
        for c in range(4):
            l_val = left if c == 0 else left * data[c - 1 : c]
            r_val = right if c == 0 else right * data[c - 1 : c]
            l_all = jnp.broadcast_to(l_val.astype(BF16), (PADS, width))
            r_all = jnp.broadcast_to(r_val.astype(BF16), (PADS, width))
            columns[c * PADS : (c + 1) * PADS] = jnp.where(
                at_left, l_all, jnp.where(at_right, r_all, nothing)
            )
        tile = (drift_pad, width)
        drift_iota = lax.broadcasted_iota(jnp.int32, tile, 0).astype(BF16)
        at_drift = jnp.where(
            drift_iota == data[7:8].astype(BF16), jnp.ones(tile, BF16), jnp.zeros(tile, BF16)
        )
        row_id = jnp.broadcast_to(data[5:6].astype(BF16), tile)
        for r in range(row_dev):
            cells[r * drift_pad : (r + 1) * drift_pad] = jnp.where(
                row_id == jnp.full(tile, r, BF16), at_drift, jnp.zeros(tile, BF16)
            )

    def add_up(cells, columns):
        hist[...] += lax.dot_general(
            cells[...], columns[...], (((1,), (1,)), ((), ())), preferred_element_type=F32
        )

    spread_out(0, cells_even, columns_even)

    def deposit(pair, _):
        later = 2 * pair + 2

        @pl.when(jnp.logical_and(later % steps == 0, later < total))
        def _():
            residual_copy(later // steps).wait_recv()

        add_up(cells_even, columns_even)
        spread_out(2 * pair + 1, cells_odd, columns_odd)
        add_up(cells_odd, columns_odd)
        spread_out(jnp.minimum(later, total - 1), cells_even, columns_even)
        return 0

    lax.fori_loop(0, total // 2, deposit, 0)

    inside = lax.broadcasted_iota(jnp.int32, (drift_pad, LANES), 1) < PAD
    sums[...] = jnp.zeros_like(sums)

    def channel(r, c):
        start = c * PADS // 128 * 128
        rows = pl.ds(pl.multiple_of(r * drift_pad, drift_pad), drift_pad)
        piece = hist[rows, start : start + LANES]
        if c * PADS != start:
            piece = pltpu.roll(piece, LANES - (c * PADS - start), 1)
        return piece

    def each_row(work, first, count):
        group = 4 if count % 4 == 0 else 1

        def some(number, _):
            for i in range(group):
                work(first + number * group + i)
            return 0

        lax.fori_loop(0, count // group, some, 0)

    def average(r):
        scale = 1.0 / (channel(r, 0) + 1.0)
        for k in range(3):
            mean = jnp.where(inside, channel(r, k + 1) * scale, 0.0)
            field[k, r + 2] = mean
            sums[k, pl.ds(r, 1)] = jnp.sum(mean, axis=0, keepdims=True)

    each_row(average, 0, row_dev)

    def across(x, weight):
        total = weight[0] * x
        for d in range(1, TAPS):
            total += weight[d] * (pltpu.roll(x, d, 1) + pltpu.roll(x, LANES - d, 1))
        return total

    def down(x):
        near = pltpu.roll(x, 1, 0) + pltpu.roll(x, rows_pad - 1, 0)
        far = pltpu.roll(x, 2, 0) + pltpu.roll(x, rows_pad - 2, 0)
        return 3.0 * x + 2.0 * near + far

    def to_low(src, dst, i):
        return pltpu.make_async_remote_copy(
            src_ref=src, dst_ref=dst, send_sem=halo_send.at[i], recv_sem=halo_recv.at[i],
            device_id={"sec": my_sec - 1}, device_id_type=MESH,
        )

    def to_high(src, dst, i):
        return pltpu.make_async_remote_copy(
            src_ref=src, dst_ref=dst, send_sem=halo_send.at[i], recv_sem=halo_recv.at[i],
            device_id={"sec": my_sec + 1}, device_id_type=MESH,
        )

    last_out[...] = jnp.zeros_like(last_out)
    for k in range(3):
        sums[k] = across(sums[k], taps)
        for j in range(2):
            last_out[0, pl.ds(k * 2 + j, 1)] = sums[k, pl.ds(j, 1)]
            last_out[1, pl.ds(k * 2 + j, 1)] = sums[k, pl.ds(row_dev - 2 + j, 1)]
    last_low = to_low(last_out.at[0], last_in.at[1], 0)
    last_high = to_high(last_out.at[1], last_in.at[0], 1)
    both_low = to_low(field.at[:, pl.ds(2, 2)], field.at[:, pl.ds(row_dev + 2, 2)], 2)
    both_high = to_high(field.at[:, pl.ds(row_dev, 2)], field.at[:, pl.ds(0, 2)], 3)

    @pl.when(has_low)
    def _():
        last_low.start()

    @pl.when(has_high)
    def _():
        last_high.start()

    @pl.when(has_high)
    def _():
        last_low.wait_recv()
        for k in range(3):
            sums[k, pl.ds(row_dev, 2)] = last_in[1, pl.ds(k * 2, 2)]

    @pl.when(has_low)
    def _():
        last_high.wait_recv()
        for k in range(3):
            sums[k, pl.ds(rows_pad - 2, 2)] = last_in[0, pl.ds(k * 2, 2)]

    totals[...] = jnp.zeros_like(totals)
    for k in range(3):
        totals[pl.ds(k * rows_pad, rows_pad)] = down(sums[k])

    def first_copy(s):
        target = lax.rem(my_gz + s, gz_count)
        return pltpu.make_async_remote_copy(
            src_ref=totals.at[pl.ds(pl.multiple_of(target * part, part), part)],
            dst_ref=by_gz.at[my_gz],
            send_sem=scan_send.at[0, s], recv_sem=scan_recv.at[0, s],
            device_id={"gz": target}, device_id_type=MESH,
        )

    def second_copy(s):
        target = lax.rem(my_tf + s, tf_count)
        return pltpu.make_async_remote_copy(
            src_ref=by_tf.at[my_tf], dst_ref=by_tf.at[my_tf],
            send_sem=scan_send.at[1, s], recv_sem=scan_recv.at[1, s],
            device_id={"tf": target}, device_id_type=MESH,
        )

    def third_copy(s):
        target = lax.rem(my_gz + s, gz_count)
        return pltpu.make_async_remote_copy(
            src_ref=back.at[target],
            dst_ref=carry.at[pl.ds(pl.multiple_of(my_gz * part, part), part)],
            send_sem=scan_send.at[2, s], recv_sem=scan_recv.at[2, s],
            device_id={"gz": target}, device_id_type=MESH,
        )

    for s in range(1, gz_count):
        first_copy(s).start()
    by_gz[my_gz] = totals[pl.ds(pl.multiple_of(my_gz * part, part), part)]

    drift_iota = lax.broadcasted_iota(jnp.int32, (drift_pad, LANES), 0)

    def widen(r):
        weight = [
            jnp.broadcast_to(taps[d, pl.ds(r, 1)], (drift_pad, LANES)) for d in range(TAPS)
        ]
        for k in range(3):
            x = across(field[k, r + 2], weight)
            d = 1
            while d < drift_dev:
                x += jnp.where(drift_iota >= d, pltpu.roll(x, d, 0), 0.0)
                d *= 2
            field[k, r + 2] = x

    for r in (0, 1, row_dev - 2, row_dev - 1):
        widen(r)

    @pl.when(has_low)
    def _():
        both_low.start()

    @pl.when(has_high)
    def _():
        both_high.start()

    early = (row_dev - 4) * 5 // 36 * 4
    each_row(widen, 2, early)

    for s in range(1, gz_count):
        first_copy(s).wait_recv()
    column = by_gz[0]
    for g in range(1, gz_count):
        column += by_gz[g]
    by_tf[my_tf] = column
    for s in range(1, tf_count):
        second_copy(s).start()
    each_row(widen, 2 + early, row_dev - 4 - early)

    for s in range(1, tf_count):
        second_copy(s).wait_recv()
    base = jnp.zeros((part, LANES), F32)
    for t in range(tf_count):
        base += jnp.where(t < my_tf, by_tf[t], 0.0)
    for g in range(gz_count):
        back[g] = base
        base = base + by_gz[g]
    for s in range(1, gz_count):
        third_copy(s).start()
    carry[pl.ds(pl.multiple_of(my_gz * part, part), part)] = back[my_gz]

    @pl.when(has_high)
    def _():
        both_low.wait_recv()

    @pl.when(has_low)
    def _():
        both_high.wait_recv()

    def finish(r):
        for k in range(3):
            near = field[k, r + 1] + field[k, r + 3]
            far = field[k, r] + field[k, r + 4]
            whole = 3.0 * field[k, r + 2] + 2.0 * near + far
            local[k, r] = whole[:drift_dev, :PAD]

    each_row(finish, 0, row_dev)
    result = pltpu.make_async_copy(local, out_ref, out_sem)
    result.start()
    for s in range(1, gz_count):
        third_copy(s).wait_recv()
    result.wait()

    for s in range(1, tf_count):
        residual_copy(s).wait_send()
        second_copy(s).wait_send()
    for s in range(1, gz_count):
        first_copy(s).wait_send()
        third_copy(s).wait_send()

    @pl.when(has_low)
    def _():
        last_low.wait_send()
        both_low.wait_send()

    @pl.when(has_high)
    def _():
        last_high.wait_send()
        both_high.wait_send()


def per_device(residuals, weights, fraction, voxels, kernel_reach):
    tf_count = lax.axis_size("tf")
    gz_count = lax.axis_size("gz")
    sec_count = lax.axis_size("sec")
    drift_dev = DRIFT // (tf_count * gz_count)
    drift_pad = round_up(drift_dev, 16)
    row_dev = kernel_reach.shape[0]
    rows_pad = round_up(row_dev + 4, 16)
    part = round_up(-(-3 * rows_pad // gz_count), 8)
    slots = weights.shape[-1]
    half = slots // 2
    step = min(1024, half)
    sizes = (
        tf_count, gz_count, sec_count, drift_dev, drift_pad, row_dev, rows_pad, part, half, step
    )
    vmem = pl.BlockSpec(memory_space=pltpu.VMEM)
    maps, carry = pl.pallas_call(
        functools.partial(kernel, sizes),
        out_shape=(
            jax.ShapeDtypeStruct((3, row_dev, drift_dev, PAD), F32),
            jax.ShapeDtypeStruct((gz_count * part, LANES), F32),
        ),
        in_specs=[vmem] * 5,
        out_specs=(pl.BlockSpec(memory_space=pl.ANY), vmem),
        scratch_shapes=[
            pltpu.VMEM((tf_count, 16, half), BF16),
            pltpu.VMEM((tf_count, 16, half), BF16),
            pltpu.VMEM((row_dev * drift_pad, 2 * step), BF16),
            pltpu.VMEM((row_dev * drift_pad, 2 * step), BF16),
            pltpu.VMEM((4 * PADS, 2 * step), BF16),
            pltpu.VMEM((4 * PADS, 2 * step), BF16),
            pltpu.VMEM((row_dev * drift_pad, 4 * PADS), F32),
            pltpu.VMEM((3, row_dev + 4, drift_pad, LANES), F32),
            pltpu.VMEM((3, rows_pad, LANES), F32),
            pltpu.VMEM((TAPS, rows_pad, LANES), F32),
            pltpu.VMEM((2, 8, LANES), F32),
            pltpu.VMEM((2, 8, LANES), F32),
            pltpu.VMEM((gz_count * part, LANES), F32),
            pltpu.VMEM((gz_count, part, LANES), F32),
            pltpu.VMEM((tf_count, part, LANES), F32),
            pltpu.VMEM((gz_count, part, LANES), F32),
            pltpu.VMEM((3, row_dev, drift_dev, PAD), F32),
            pltpu.SemaphoreType.DMA((tf_count,)),
            pltpu.SemaphoreType.DMA((tf_count,)),
            pltpu.SemaphoreType.DMA((4,)),
            pltpu.SemaphoreType.DMA((4,)),
            pltpu.SemaphoreType.DMA((3, max(tf_count, gz_count))),
            pltpu.SemaphoreType.DMA((3, max(tf_count, gz_count))),
            pltpu.SemaphoreType.DMA,
        ],
        compiler_params=pltpu.CompilerParams(
            collective_id=0, has_side_effects=True, vmem_limit_bytes=56 * 1024 * 1024
        ),
    )(
        residuals[:, 0, 0, 0],
        weights[0, 0, 0],
        fraction[0, 0, 0],
        voxels[:, 0, 0, 0],
        kernel_reach[None, :],
    )
    carry = carry[: 3 * rows_pad].reshape(3, rows_pad, LANES)[:, :row_dev, :PAD]
    return jnp.transpose(maps + carry[:, :, None], (0, 2, 1, 3))


def solution(mesh):
    placed = (
        P(None, "tf", "gz", "sec", None, None),
        P("tf", "gz", "sec", None, None),
        P("tf", "gz", "sec", None, None),
        P(None, "tf", "gz", "sec", None, None),
        P("sec"),
    )
    return jax.shard_map(
        per_device,
        mesh=mesh,
        in_specs=placed,
        out_specs=P(None, ("tf", "gz"), "sec", None),
        check_vma=False,
    )
```

```python
import functools

import jax
import jax.numpy as jnp
from jax import lax
from jax.experimental import pallas as pl
from jax.experimental.pallas import tpu as pltpu
from jax.sharding import PartitionSpec as P

PAD = 180
DRIFT = 256
PADS = 192
LANES = 256
TAPS = 5
MESH = pl.DeviceIdType.MESH
F32 = jnp.float32
BF16 = jnp.bfloat16


def round_up(value, unit):
    return (value + unit - 1) // unit * unit


def kernel(
    sizes,
    res_ref,
    weight_ref,
    frac_ref,
    vox_ref,
    reach_ref,
    out_ref,
    carry_ref,
    send_buf,
    recv_buf,
    cells_even,
    cells_odd,
    columns_even,
    columns_odd,
    hist,
    field,
    sums,
    taps,
    last_out,
    last_in,
    totals,
    by_gz,
    by_tf,
    back,
    carry,
    local,
    res_send,
    res_recv,
    halo_send,
    halo_recv,
    scan_send,
    scan_recv,
    out_sem,
):
    tf_count, gz_count, sec_count, drift_dev, drift_pad, row_dev, rows_pad, part, half, step = sizes
    my_tf = lax.axis_index("tf")
    my_gz = lax.axis_index("gz")
    my_sec = lax.axis_index("sec")
    has_low = my_sec > 0
    has_high = my_sec < sec_count - 1

    for r in (0, 1, row_dev + 2, row_dev + 3):
        field[:, r] = jnp.zeros((3, drift_pad, LANES), F32)

    barrier = pltpu.get_barrier_semaphore()
    for s in range(1, tf_count):
        pl.semaphore_signal(
            barrier, inc=1, device_id={"tf": lax.rem(my_tf + s, tf_count)}, device_id_type=MESH
        )
    for s in range(1, gz_count):
        pl.semaphore_signal(
            barrier, inc=1, device_id={"gz": lax.rem(my_gz + s, gz_count)}, device_id_type=MESH
        )

    @pl.when(has_low)
    def _():
        pl.semaphore_signal(barrier, inc=1, device_id={"sec": my_sec - 1}, device_id_type=MESH)

    @pl.when(has_high)
    def _():
        pl.semaphore_signal(barrier, inc=1, device_id={"sec": my_sec + 1}, device_id_type=MESH)

    first_row = my_sec * row_dev
    channels = [res_ref[0], res_ref[1], res_ref[2], weight_ref[...], frac_ref[...]]
    channels = [c.astype(F32) for c in channels]
    channels.append((vox_ref[0] - first_row).astype(F32))
    channels.append(vox_ref[1].astype(F32))
    block_of = lax.broadcasted_iota(jnp.int32, vox_ref.shape[1:], 0)
    channels.append((vox_ref[2] - (block_of * gz_count + my_gz) * drift_dev).astype(F32))
    for t in range(tf_count):
        rows = [c[t : t + 1, h * half : (h + 1) * half] for h in range(2) for c in channels]
        send_buf[t] = jnp.concatenate(rows, axis=0).astype(BF16)

    neighbours = has_low.astype(jnp.int32) + has_high.astype(jnp.int32)
    pl.semaphore_wait(barrier, tf_count + gz_count - 2 + neighbours)

    def residual_copy(s):
        target = lax.rem(my_tf + s, tf_count)
        return pltpu.make_async_remote_copy(
            src_ref=send_buf.at[target],
            dst_ref=recv_buf.at[s],
            send_sem=res_send.at[s],
            recv_sem=res_recv.at[s],
            device_id={"tf": target},
            device_id_type=MESH,
        )

    for s in range(1, tf_count):
        residual_copy(s).start()
    recv_buf[0] = send_buf[my_tf]
    hist[...] = jnp.zeros_like(hist)

    square = (rows_pad, row_dev)
    diagonal = lax.broadcasted_iota(jnp.int32, square, 0) == lax.broadcasted_iota(
        jnp.int32, square, 1
    )
    reach = jnp.broadcast_to(reach_ref[...].astype(F32), square)
    reach = jnp.sum(jnp.where(diagonal, reach, 0.0), axis=1, keepdims=True)
    spread = jnp.broadcast_to(reach, (rows_pad, LANES)) + 1.0
    for d in range(TAPS):
        taps[d] = jnp.maximum(spread - float(d), 0.0) / (spread * spread * 9.0)

    steps = half // step
    width = 2 * step

    total = tf_count * steps

    def spread_out(number, cells, columns):
        s = number // steps
        j = number % steps
        block = recv_buf[s, :, pl.ds(pl.multiple_of(j * step, step), step)].astype(F32)
        data = jnp.concatenate([block[0:8], block[8:16]], axis=1)
        left = data[3:4] * (1.0 - data[4:5])
        right = data[3:4] * data[4:5]
        pad_id = data[6:7].astype(BF16)
        next_id = (data[6:7] + 1.0).astype(BF16)
        pad_iota = lax.broadcasted_iota(jnp.int32, (PADS, width), 0).astype(BF16)
        at_left = pad_iota == pad_id
        at_right = pad_iota == next_id
        nothing = jnp.zeros((PADS, width), BF16)
        for c in range(4):
            l_val = left if c == 0 else left * data[c - 1 : c]
            r_val = right if c == 0 else right * data[c - 1 : c]
            l_all = jnp.broadcast_to(l_val.astype(BF16), (PADS, width))
            r_all = jnp.broadcast_to(r_val.astype(BF16), (PADS, width))
            columns[c * PADS : (c + 1) * PADS] = jnp.where(
                at_left, l_all, jnp.where(at_right, r_all, nothing)
            )
        tile = (drift_pad, width)
        drift_iota = lax.broadcasted_iota(jnp.int32, tile, 0).astype(BF16)
        at_drift = jnp.where(
            drift_iota == data[7:8].astype(BF16), jnp.ones(tile, BF16), jnp.zeros(tile, BF16)
        )
        row_id = jnp.broadcast_to(data[5:6].astype(BF16), tile)
        for r in range(row_dev):
            cells[r * drift_pad : (r + 1) * drift_pad] = jnp.where(
                row_id == jnp.full(tile, r, BF16), at_drift, jnp.zeros(tile, BF16)
            )

    def add_up(cells, columns):
        hist[...] += lax.dot_general(
            cells[...], columns[...], (((1,), (1,)), ((), ())), preferred_element_type=F32
        )

    spread_out(0, cells_even, columns_even)

    def deposit(pair, _):
        later = 2 * pair + 2

        @pl.when(jnp.logical_and(later % steps == 0, later < total))
        def _():
            residual_copy(later // steps).wait_recv()

        add_up(cells_even, columns_even)
        spread_out(2 * pair + 1, cells_odd, columns_odd)
        add_up(cells_odd, columns_odd)
        spread_out(jnp.minimum(later, total - 1), cells_even, columns_even)
        return 0

    lax.fori_loop(0, total // 2, deposit, 0)

    inside = lax.broadcasted_iota(jnp.int32, (drift_pad, LANES), 1) < PAD
    sums[...] = jnp.zeros_like(sums)

    def channel(r, c):
        start = c * PADS // 128 * 128
        rows = pl.ds(pl.multiple_of(r * drift_pad, drift_pad), drift_pad)
        piece = hist[rows, start : start + LANES]
        if c * PADS != start:
            piece = pltpu.roll(piece, LANES - (c * PADS - start), 1)
        return piece

    def each_row(work, first, count):
        group = 4 if count % 4 == 0 else 1

        def some(number, _):
            for i in range(group):
                work(first + number * group + i)
            return 0

        lax.fori_loop(0, count // group, some, 0)

    def average(r):
        scale = 1.0 / (channel(r, 0) + 1.0)
        for k in range(3):
            mean = jnp.where(inside, channel(r, k + 1) * scale, 0.0)
            field[k, r + 2] = mean
            sums[k, pl.ds(r, 1)] = jnp.sum(mean, axis=0, keepdims=True)

    each_row(average, 0, row_dev)

    def across(x, weight):
        total = weight[0] * x
        for d in range(1, TAPS):
            total += weight[d] * (pltpu.roll(x, d, 1) + pltpu.roll(x, LANES - d, 1))
        return total

    def down(x):
        near = pltpu.roll(x, 1, 0) + pltpu.roll(x, rows_pad - 1, 0)
        far = pltpu.roll(x, 2, 0) + pltpu.roll(x, rows_pad - 2, 0)
        return 3.0 * x + 2.0 * near + far

    def to_low(src, dst, i):
        return pltpu.make_async_remote_copy(
            src_ref=src, dst_ref=dst, send_sem=halo_send.at[i], recv_sem=halo_recv.at[i],
            device_id={"sec": my_sec - 1}, device_id_type=MESH,
        )

    def to_high(src, dst, i):
        return pltpu.make_async_remote_copy(
            src_ref=src, dst_ref=dst, send_sem=halo_send.at[i], recv_sem=halo_recv.at[i],
            device_id={"sec": my_sec + 1}, device_id_type=MESH,
        )

    last_out[...] = jnp.zeros_like(last_out)
    for k in range(3):
        sums[k] = across(sums[k], taps)
        for j in range(2):
            last_out[0, pl.ds(k * 2 + j, 1)] = sums[k, pl.ds(j, 1)]
            last_out[1, pl.ds(k * 2 + j, 1)] = sums[k, pl.ds(row_dev - 2 + j, 1)]
    last_low = to_low(last_out.at[0], last_in.at[1], 0)
    last_high = to_high(last_out.at[1], last_in.at[0], 1)
    both_low = to_low(field.at[:, pl.ds(2, 2)], field.at[:, pl.ds(row_dev + 2, 2)], 2)
    both_high = to_high(field.at[:, pl.ds(row_dev, 2)], field.at[:, pl.ds(0, 2)], 3)

    @pl.when(has_low)
    def _():
        last_low.start()

    @pl.when(has_high)
    def _():
        last_high.start()

    @pl.when(has_high)
    def _():
        last_low.wait_recv()
        for k in range(3):
            sums[k, pl.ds(row_dev, 2)] = last_in[1, pl.ds(k * 2, 2)]

    @pl.when(has_low)
    def _():
        last_high.wait_recv()
        for k in range(3):
            sums[k, pl.ds(rows_pad - 2, 2)] = last_in[0, pl.ds(k * 2, 2)]

    all_rows = 3 * rows_pad
    mid = all_rows // 2
    whole_sums = jnp.concatenate([down(sums[k]) for k in range(3)], axis=0)
    totals[...] = jnp.zeros_like(totals)
    totals[:all_rows] = whole_sums[:, :128]
    upper = whole_sums[:, 128:]
    pair_lane = lax.broadcasted_iota(jnp.int32, (mid, 128), 1)
    totals[all_rows : all_rows + mid] = jnp.where(
        pair_lane < 64, upper[:mid], pltpu.roll(upper[mid:], 64, 1)
    )

    def first_copy(s):
        target = lax.rem(my_gz + s, gz_count)
        return pltpu.make_async_remote_copy(
            src_ref=totals.at[pl.ds(pl.multiple_of(target * part, part), part)],
            dst_ref=by_gz.at[my_gz],
            send_sem=scan_send.at[0, s], recv_sem=scan_recv.at[0, s],
            device_id={"gz": target}, device_id_type=MESH,
        )

    def second_copy(s):
        target = lax.rem(my_tf + s, tf_count)
        return pltpu.make_async_remote_copy(
            src_ref=by_tf.at[my_tf], dst_ref=by_tf.at[my_tf],
            send_sem=scan_send.at[1, s], recv_sem=scan_recv.at[1, s],
            device_id={"tf": target}, device_id_type=MESH,
        )

    def third_copy(s):
        target = lax.rem(my_gz + s, gz_count)
        return pltpu.make_async_remote_copy(
            src_ref=back.at[target],
            dst_ref=carry.at[pl.ds(pl.multiple_of(my_gz * part, part), part)],
            send_sem=scan_send.at[2, s], recv_sem=scan_recv.at[2, s],
            device_id={"gz": target}, device_id_type=MESH,
        )

    for s in range(1, gz_count):
        first_copy(s).start()
    by_gz[my_gz] = totals[pl.ds(pl.multiple_of(my_gz * part, part), part)]

    drift_iota = lax.broadcasted_iota(jnp.int32, (drift_pad, LANES), 0)

    def widen(r):
        weight = [
            jnp.broadcast_to(taps[d, pl.ds(r, 1)], (drift_pad, LANES)) for d in range(TAPS)
        ]
        for k in range(3):
            x = across(field[k, r + 2], weight)
            d = 1
            while d < drift_dev:
                x += jnp.where(drift_iota >= d, pltpu.roll(x, d, 0), 0.0)
                d *= 2
            field[k, r + 2] = x

    for r in (0, 1, row_dev - 2, row_dev - 1):
        widen(r)

    @pl.when(has_low)
    def _():
        both_low.start()

    @pl.when(has_high)
    def _():
        both_high.start()

    early = (row_dev - 4) * 5 // 36 * 4
    each_row(widen, 2, early)

    for s in range(1, gz_count):
        first_copy(s).wait_recv()
    column = by_gz[0]
    for g in range(1, gz_count):
        column += by_gz[g]
    by_tf[my_tf] = column
    for s in range(1, tf_count):
        second_copy(s).start()
    each_row(widen, 2 + early, row_dev - 4 - early)

    for s in range(1, tf_count):
        second_copy(s).wait_recv()
    base = jnp.zeros((part, 128), F32)
    for t in range(tf_count):
        base += jnp.where(t < my_tf, by_tf[t], 0.0)
    for g in range(gz_count):
        back[g] = base
        base = base + by_gz[g]
    for s in range(1, gz_count):
        third_copy(s).start()
    carry[pl.ds(pl.multiple_of(my_gz * part, part), part)] = back[my_gz]

    @pl.when(has_high)
    def _():
        both_low.wait_recv()

    @pl.when(has_low)
    def _():
        both_high.wait_recv()

    def finish(r):
        for k in range(3):
            near = field[k, r + 1] + field[k, r + 3]
            far = field[k, r] + field[k, r + 4]
            whole = 3.0 * field[k, r + 2] + 2.0 * near + far
            local[k, r] = whole[:drift_dev, :PAD]

    each_row(finish, 0, row_dev)
    result = pltpu.make_async_copy(local, out_ref, out_sem)
    result.start()
    for s in range(1, gz_count):
        third_copy(s).wait_recv()
    pairs = carry[all_rows : all_rows + mid]
    upper = jnp.concatenate([pairs, pltpu.roll(pairs, 64, 1)], axis=0)
    for k in range(3):
        rows = slice(k * rows_pad, k * rows_pad + row_dev)
        carry_ref[k, :, :128] = carry[rows]
        carry_ref[k, :, 128:] = upper[rows, : PAD - 128]
    result.wait()

    for s in range(1, tf_count):
        residual_copy(s).wait_send()
        second_copy(s).wait_send()
    for s in range(1, gz_count):
        first_copy(s).wait_send()
        third_copy(s).wait_send()

    @pl.when(has_low)
    def _():
        last_low.wait_send()
        both_low.wait_send()

    @pl.when(has_high)
    def _():
        last_high.wait_send()
        both_high.wait_send()


def per_device(residuals, weights, fraction, voxels, kernel_reach):
    tf_count = lax.axis_size("tf")
    gz_count = lax.axis_size("gz")
    sec_count = lax.axis_size("sec")
    drift_dev = DRIFT // (tf_count * gz_count)
    drift_pad = round_up(drift_dev, 16)
    row_dev = kernel_reach.shape[0]
    rows_pad = round_up(row_dev + 4, 16)
    part = round_up(-(-9 * rows_pad // (2 * gz_count)), 8)
    slots = weights.shape[-1]
    half = slots // 2
    step = min(1024, half)
    sizes = (
        tf_count, gz_count, sec_count, drift_dev, drift_pad, row_dev, rows_pad, part, half, step
    )
    vmem = pl.BlockSpec(memory_space=pltpu.VMEM)
    maps, carry = pl.pallas_call(
        functools.partial(kernel, sizes),
        out_shape=(
            jax.ShapeDtypeStruct((3, row_dev, drift_dev, PAD), F32),
            jax.ShapeDtypeStruct((3, row_dev, PAD), F32),
        ),
        in_specs=[vmem] * 5,
        out_specs=(pl.BlockSpec(memory_space=pl.ANY), vmem),
        scratch_shapes=[
            pltpu.VMEM((tf_count, 16, half), BF16),
            pltpu.VMEM((tf_count, 16, half), BF16),
            pltpu.VMEM((row_dev * drift_pad, 2 * step), BF16),
            pltpu.VMEM((row_dev * drift_pad, 2 * step), BF16),
            pltpu.VMEM((4 * PADS, 2 * step), BF16),
            pltpu.VMEM((4 * PADS, 2 * step), BF16),
            pltpu.VMEM((row_dev * drift_pad, 4 * PADS), F32),
            pltpu.VMEM((3, row_dev + 4, drift_pad, LANES), F32),
            pltpu.VMEM((3, rows_pad, LANES), F32),
            pltpu.VMEM((TAPS, rows_pad, LANES), F32),
            pltpu.VMEM((2, 8, LANES), F32),
            pltpu.VMEM((2, 8, LANES), F32),
            pltpu.VMEM((gz_count * part, 128), F32),
            pltpu.VMEM((gz_count, part, 128), F32),
            pltpu.VMEM((tf_count, part, 128), F32),
            pltpu.VMEM((gz_count, part, 128), F32),
            pltpu.VMEM((gz_count * part, 128), F32),
            pltpu.VMEM((3, row_dev, drift_dev, PAD), F32),
            pltpu.SemaphoreType.DMA((tf_count,)),
            pltpu.SemaphoreType.DMA((tf_count,)),
            pltpu.SemaphoreType.DMA((4,)),
            pltpu.SemaphoreType.DMA((4,)),
            pltpu.SemaphoreType.DMA((3, max(tf_count, gz_count))),
            pltpu.SemaphoreType.DMA((3, max(tf_count, gz_count))),
            pltpu.SemaphoreType.DMA,
        ],
        compiler_params=pltpu.CompilerParams(
            collective_id=0, has_side_effects=True, vmem_limit_bytes=40 * 1024 * 1024
        ),
    )(
        residuals[:, 0, 0, 0],
        weights[0, 0, 0],
        fraction[0, 0, 0],
        voxels[:, 0, 0, 0],
        kernel_reach[None, :],
    )
    return jnp.transpose(maps + carry[:, :, None], (0, 2, 1, 3))


def solution(mesh):
    placed = (
        P(None, "tf", "gz", "sec", None, None),
        P("tf", "gz", "sec", None, None),
        P("tf", "gz", "sec", None, None),
        P(None, "tf", "gz", "sec", None, None),
        P("sec"),
    )
    return jax.shard_map(
        per_device,
        mesh=mesh,
        in_specs=placed,
        out_specs=P(None, ("tf", "gz"), "sec", None),
        check_vma=False,
    )
```

```python
import functools

import jax
import jax.numpy as jnp
from jax import lax
from jax.experimental import pallas as pl
from jax.experimental.pallas import tpu as pltpu
from jax.sharding import PartitionSpec as P

PAD = 180
DRIFT = 256
PADS = 192
LANES = 256
TAPS = 5
MESH = pl.DeviceIdType.MESH
F32 = jnp.float32
BF16 = jnp.bfloat16


def round_up(value, unit):
    return (value + unit - 1) // unit * unit


def kernel(
    sizes,
    res_ref,
    weight_ref,
    frac_ref,
    vox_ref,
    reach_ref,
    out_ref,
    carry_ref,
    send_buf,
    recv_buf,
    cells_even,
    cells_odd,
    columns_even,
    columns_odd,
    hist,
    field,
    sums,
    taps,
    last_out,
    last_in,
    totals,
    by_gz,
    by_tf,
    back,
    carry,
    local,
    res_send,
    res_recv,
    halo_send,
    halo_recv,
    scan_send,
    scan_recv,
    out_sem,
):
    tf_count, gz_count, sec_count, drift_dev, drift_pad, row_dev, rows_pad, part, half, step = sizes
    my_tf = lax.axis_index("tf")
    my_gz = lax.axis_index("gz")
    my_sec = lax.axis_index("sec")
    has_low = my_sec > 0
    has_high = my_sec < sec_count - 1

    for r in (0, 1, row_dev + 2, row_dev + 3):
        field[:, r] = jnp.zeros((3, drift_pad, LANES), F32)

    barrier = pltpu.get_barrier_semaphore()
    for s in range(1, tf_count):
        pl.semaphore_signal(
            barrier, inc=1, device_id={"tf": lax.rem(my_tf + s, tf_count)}, device_id_type=MESH
        )
    for s in range(1, gz_count):
        pl.semaphore_signal(
            barrier, inc=1, device_id={"gz": lax.rem(my_gz + s, gz_count)}, device_id_type=MESH
        )

    @pl.when(has_low)
    def _():
        pl.semaphore_signal(barrier, inc=1, device_id={"sec": my_sec - 1}, device_id_type=MESH)

    @pl.when(has_high)
    def _():
        pl.semaphore_signal(barrier, inc=1, device_id={"sec": my_sec + 1}, device_id_type=MESH)

    first_row = my_sec * row_dev
    channels = [res_ref[0], res_ref[1], res_ref[2], weight_ref[...], frac_ref[...]]
    channels = [c.astype(F32) for c in channels]
    channels.append((vox_ref[0] - first_row).astype(F32))
    channels.append(vox_ref[1].astype(F32))
    block_of = lax.broadcasted_iota(jnp.int32, vox_ref.shape[1:], 0)
    channels.append((vox_ref[2] - (block_of * gz_count + my_gz) * drift_dev).astype(F32))
    for t in range(tf_count):
        rows = [c[t : t + 1, h * half : (h + 1) * half] for h in range(2) for c in channels]
        send_buf[t] = jnp.concatenate(rows, axis=0).astype(BF16)

    neighbours = has_low.astype(jnp.int32) + has_high.astype(jnp.int32)
    pl.semaphore_wait(barrier, tf_count + gz_count - 2 + neighbours)

    def residual_copy(s):
        target = lax.rem(my_tf + s, tf_count)
        return pltpu.make_async_remote_copy(
            src_ref=send_buf.at[target],
            dst_ref=recv_buf.at[s],
            send_sem=res_send.at[s],
            recv_sem=res_recv.at[s],
            device_id={"tf": target},
            device_id_type=MESH,
        )

    for s in range(1, tf_count):
        residual_copy(s).start()
    recv_buf[0] = send_buf[my_tf]
    hist[...] = jnp.zeros_like(hist)

    square = (rows_pad, row_dev)
    diagonal = lax.broadcasted_iota(jnp.int32, square, 0) == lax.broadcasted_iota(
        jnp.int32, square, 1
    )
    reach = jnp.broadcast_to(reach_ref[...].astype(F32), square)
    reach = jnp.sum(jnp.where(diagonal, reach, 0.0), axis=1, keepdims=True)
    spread = jnp.broadcast_to(reach, (rows_pad, LANES)) + 1.0
    for d in range(TAPS):
        taps[d] = jnp.maximum(spread - float(d), 0.0) / (spread * spread * 9.0)

    steps = half // step
    width = 2 * step

    total = tf_count * steps

    def spread_out(number, cells, columns):
        s = number // steps
        j = number % steps
        block = recv_buf[s, :, pl.ds(pl.multiple_of(j * step, step), step)].astype(F32)
        data = jnp.concatenate([block[0:8], block[8:16]], axis=1)
        left = data[3:4] * (1.0 - data[4:5])
        right = data[3:4] * data[4:5]
        pad_id = data[6:7].astype(BF16)
        next_id = (data[6:7] + 1.0).astype(BF16)
        pad_iota = lax.broadcasted_iota(jnp.int32, (PADS, width), 0).astype(BF16)
        at_left = pad_iota == pad_id
        at_right = pad_iota == next_id
        nothing = jnp.zeros((PADS, width), BF16)
        for c in range(4):
            l_val = left if c == 0 else left * data[c - 1 : c]
            r_val = right if c == 0 else right * data[c - 1 : c]
            l_all = jnp.broadcast_to(l_val.astype(BF16), (PADS, width))
            r_all = jnp.broadcast_to(r_val.astype(BF16), (PADS, width))
            columns[c * PADS : (c + 1) * PADS] = jnp.where(
                at_left, l_all, jnp.where(at_right, r_all, nothing)
            )
        tile = (drift_pad, width)
        drift_iota = lax.broadcasted_iota(jnp.int32, tile, 0).astype(BF16)
        at_drift = jnp.where(
            drift_iota == data[7:8].astype(BF16), jnp.ones(tile, BF16), jnp.zeros(tile, BF16)
        )
        row_id = jnp.broadcast_to(data[5:6].astype(BF16), tile)
        for r in range(row_dev):
            cells[r * drift_pad : (r + 1) * drift_pad] = jnp.where(
                row_id == jnp.full(tile, r, BF16), at_drift, jnp.zeros(tile, BF16)
            )

    def add_up(cells, columns):
        hist[...] += lax.dot_general(
            cells[...], columns[...], (((1,), (1,)), ((), ())), preferred_element_type=F32
        )

    spread_out(0, cells_even, columns_even)

    def deposit(pair, _):
        later = 2 * pair + 2

        @pl.when(later % steps == 0)
        def _():
            residual_copy(later // steps).wait_recv()

        add_up(cells_even, columns_even)
        spread_out(2 * pair + 1, cells_odd, columns_odd)
        add_up(cells_odd, columns_odd)
        spread_out(later, cells_even, columns_even)
        return 0

    lax.fori_loop(0, total // 2 - 1, deposit, 0)
    add_up(cells_even, columns_even)
    spread_out(total - 1, cells_odd, columns_odd)
    add_up(cells_odd, columns_odd)

    inside = lax.broadcasted_iota(jnp.int32, (drift_pad, LANES), 1) < PAD
    sums[...] = jnp.zeros_like(sums)

    def channel(r, c):
        start = c * PADS // 128 * 128
        rows = pl.ds(pl.multiple_of(r * drift_pad, drift_pad), drift_pad)
        piece = hist[rows, start : start + LANES]
        if c * PADS != start:
            piece = pltpu.roll(piece, LANES - (c * PADS - start), 1)
        return piece

    def each_row(work, first, count):
        group = 4 if count % 4 == 0 else 1

        def some(number, _):
            for i in range(group):
                work(first + number * group + i)
            return 0

        lax.fori_loop(0, count // group, some, 0)

    def average(r):
        scale = 1.0 / (channel(r, 0) + 1.0)
        for k in range(3):
            mean = jnp.where(inside, channel(r, k + 1) * scale, 0.0)
            field[k, r + 2] = mean
            sums[k, pl.ds(r, 1)] = jnp.sum(mean, axis=0, keepdims=True)

    each_row(average, 0, row_dev)

    def across(x, weight):
        total = weight[0] * x
        for d in range(1, TAPS):
            total += weight[d] * (pltpu.roll(x, d, 1) + pltpu.roll(x, LANES - d, 1))
        return total

    def down(x):
        near = pltpu.roll(x, 1, 0) + pltpu.roll(x, rows_pad - 1, 0)
        far = pltpu.roll(x, 2, 0) + pltpu.roll(x, rows_pad - 2, 0)
        return 3.0 * x + 2.0 * near + far

    def to_low(src, dst, i):
        return pltpu.make_async_remote_copy(
            src_ref=src, dst_ref=dst, send_sem=halo_send.at[i], recv_sem=halo_recv.at[i],
            device_id={"sec": my_sec - 1}, device_id_type=MESH,
        )

    def to_high(src, dst, i):
        return pltpu.make_async_remote_copy(
            src_ref=src, dst_ref=dst, send_sem=halo_send.at[i], recv_sem=halo_recv.at[i],
            device_id={"sec": my_sec + 1}, device_id_type=MESH,
        )

    last_out[...] = jnp.zeros_like(last_out)
    for k in range(3):
        sums[k] = across(sums[k], taps)
        for j in range(2):
            last_out[0, pl.ds(k * 2 + j, 1)] = sums[k, pl.ds(j, 1)]
            last_out[1, pl.ds(k * 2 + j, 1)] = sums[k, pl.ds(row_dev - 2 + j, 1)]
    last_low = to_low(last_out.at[0], last_in.at[1], 0)
    last_high = to_high(last_out.at[1], last_in.at[0], 1)
    both_low = to_low(field.at[:, pl.ds(2, 2)], field.at[:, pl.ds(row_dev + 2, 2)], 2)
    both_high = to_high(field.at[:, pl.ds(row_dev, 2)], field.at[:, pl.ds(0, 2)], 3)

    @pl.when(has_low)
    def _():
        last_low.start()

    @pl.when(has_high)
    def _():
        last_high.start()

    @pl.when(has_high)
    def _():
        last_low.wait_recv()
        for k in range(3):
            sums[k, pl.ds(row_dev, 2)] = last_in[1, pl.ds(k * 2, 2)]

    @pl.when(has_low)
    def _():
        last_high.wait_recv()
        for k in range(3):
            sums[k, pl.ds(rows_pad - 2, 2)] = last_in[0, pl.ds(k * 2, 2)]

    all_rows = 3 * rows_pad
    mid = all_rows // 2
    whole_sums = jnp.concatenate([down(sums[k]) for k in range(3)], axis=0)
    totals[...] = jnp.zeros_like(totals)
    totals[:all_rows] = whole_sums[:, :128]
    upper = whole_sums[:, 128:]
    pair_lane = lax.broadcasted_iota(jnp.int32, (mid, 128), 1)
    totals[all_rows : all_rows + mid] = jnp.where(
        pair_lane < 64, upper[:mid], pltpu.roll(upper[mid:], 64, 1)
    )

    def first_copy(s):
        target = lax.rem(my_gz + s, gz_count)
        return pltpu.make_async_remote_copy(
            src_ref=totals.at[pl.ds(pl.multiple_of(target * part, part), part)],
            dst_ref=by_gz.at[my_gz],
            send_sem=scan_send.at[0, s], recv_sem=scan_recv.at[0, s],
            device_id={"gz": target}, device_id_type=MESH,
        )

    def second_copy(s):
        target = lax.rem(my_tf + s, tf_count)
        return pltpu.make_async_remote_copy(
            src_ref=by_tf.at[my_tf], dst_ref=by_tf.at[my_tf],
            send_sem=scan_send.at[1, s], recv_sem=scan_recv.at[1, s],
            device_id={"tf": target}, device_id_type=MESH,
        )

    def third_copy(s):
        target = lax.rem(my_gz + s, gz_count)
        return pltpu.make_async_remote_copy(
            src_ref=back.at[target],
            dst_ref=carry.at[pl.ds(pl.multiple_of(my_gz * part, part), part)],
            send_sem=scan_send.at[2, s], recv_sem=scan_recv.at[2, s],
            device_id={"gz": target}, device_id_type=MESH,
        )

    for s in range(1, gz_count):
        first_copy(s).start()
    by_gz[my_gz] = totals[pl.ds(pl.multiple_of(my_gz * part, part), part)]

    drift_iota = lax.broadcasted_iota(jnp.int32, (drift_pad, LANES), 0)

    def widen(r):
        weight = [
            jnp.broadcast_to(taps[d, pl.ds(r, 1)], (drift_pad, LANES)) for d in range(TAPS)
        ]
        for k in range(3):
            x = across(field[k, r + 2], weight)
            d = 1
            while d < drift_dev:
                x += jnp.where(drift_iota >= d, pltpu.roll(x, d, 0), 0.0)
                d *= 2
            field[k, r + 2] = x

    for r in (0, 1, row_dev - 2, row_dev - 1):
        widen(r)

    @pl.when(has_low)
    def _():
        both_low.start()

    @pl.when(has_high)
    def _():
        both_high.start()

    early = (row_dev - 4) * 5 // 36 * 4
    each_row(widen, 2, early)

    for s in range(1, gz_count):
        first_copy(s).wait_recv()
    column = by_gz[0]
    for g in range(1, gz_count):
        column += by_gz[g]
    by_tf[my_tf] = column
    for s in range(1, tf_count):
        second_copy(s).start()
    each_row(widen, 2 + early, row_dev - 4 - early)

    for s in range(1, tf_count):
        second_copy(s).wait_recv()
    base = jnp.zeros((part, 128), F32)
    for t in range(tf_count):
        base += jnp.where(t < my_tf, by_tf[t], 0.0)
    for g in range(gz_count):
        back[g] = base
        base = base + by_gz[g]
    for s in range(1, gz_count):
        third_copy(s).start()
    carry[pl.ds(pl.multiple_of(my_gz * part, part), part)] = back[my_gz]

    @pl.when(has_high)
    def _():
        both_low.wait_recv()

    @pl.when(has_low)
    def _():
        both_high.wait_recv()

    def finish(r):
        for k in range(3):
            near = field[k, r + 1] + field[k, r + 3]
            far = field[k, r] + field[k, r + 4]
            whole = 3.0 * field[k, r + 2] + 2.0 * near + far
            local[k, r] = whole[:drift_dev, :PAD]

    each_row(finish, 0, row_dev)
    result = pltpu.make_async_copy(local, out_ref, out_sem)
    result.start()
    for s in range(1, gz_count):
        third_copy(s).wait_recv()
    pairs = carry[all_rows : all_rows + mid]
    upper = jnp.concatenate([pairs, pltpu.roll(pairs, 64, 1)], axis=0)
    for k in range(3):
        rows = slice(k * rows_pad, k * rows_pad + row_dev)
        carry_ref[k, :, :128] = carry[rows]
        carry_ref[k, :, 128:] = upper[rows, : PAD - 128]
    result.wait()

    for s in range(1, tf_count):
        residual_copy(s).wait_send()
        second_copy(s).wait_send()
    for s in range(1, gz_count):
        first_copy(s).wait_send()
        third_copy(s).wait_send()

    @pl.when(has_low)
    def _():
        last_low.wait_send()
        both_low.wait_send()

    @pl.when(has_high)
    def _():
        last_high.wait_send()
        both_high.wait_send()


def per_device(residuals, weights, fraction, voxels, kernel_reach):
    tf_count = lax.axis_size("tf")
    gz_count = lax.axis_size("gz")
    sec_count = lax.axis_size("sec")
    drift_dev = DRIFT // (tf_count * gz_count)
    drift_pad = round_up(drift_dev, 16)
    row_dev = kernel_reach.shape[0]
    rows_pad = round_up(row_dev + 4, 16)
    part = round_up(-(-9 * rows_pad // (2 * gz_count)), 8)
    slots = weights.shape[-1]
    half = slots // 2
    step = min(1024, half)
    sizes = (
        tf_count, gz_count, sec_count, drift_dev, drift_pad, row_dev, rows_pad, part, half, step
    )
    vmem = pl.BlockSpec(memory_space=pltpu.VMEM)
    maps, carry = pl.pallas_call(
        functools.partial(kernel, sizes),
        out_shape=(
            jax.ShapeDtypeStruct((3, row_dev, drift_dev, PAD), F32),
            jax.ShapeDtypeStruct((3, row_dev, PAD), F32),
        ),
        in_specs=[vmem] * 5,
        out_specs=(pl.BlockSpec(memory_space=pl.ANY), vmem),
        scratch_shapes=[
            pltpu.VMEM((tf_count, 16, half), BF16),
            pltpu.VMEM((tf_count, 16, half), BF16),
            pltpu.VMEM((row_dev * drift_pad, 2 * step), BF16),
            pltpu.VMEM((row_dev * drift_pad, 2 * step), BF16),
            pltpu.VMEM((4 * PADS, 2 * step), BF16),
            pltpu.VMEM((4 * PADS, 2 * step), BF16),
            pltpu.VMEM((row_dev * drift_pad, 4 * PADS), F32),
            pltpu.VMEM((3, row_dev + 4, drift_pad, LANES), F32),
            pltpu.VMEM((3, rows_pad, LANES), F32),
            pltpu.VMEM((TAPS, rows_pad, LANES), F32),
            pltpu.VMEM((2, 8, LANES), F32),
            pltpu.VMEM((2, 8, LANES), F32),
            pltpu.VMEM((gz_count * part, 128), F32),
            pltpu.VMEM((gz_count, part, 128), F32),
            pltpu.VMEM((tf_count, part, 128), F32),
            pltpu.VMEM((gz_count, part, 128), F32),
            pltpu.VMEM((gz_count * part, 128), F32),
            pltpu.VMEM((3, row_dev, drift_dev, PAD), F32),
            pltpu.SemaphoreType.DMA((tf_count,)),
            pltpu.SemaphoreType.DMA((tf_count,)),
            pltpu.SemaphoreType.DMA((4,)),
            pltpu.SemaphoreType.DMA((4,)),
            pltpu.SemaphoreType.DMA((3, max(tf_count, gz_count))),
            pltpu.SemaphoreType.DMA((3, max(tf_count, gz_count))),
            pltpu.SemaphoreType.DMA,
        ],
        compiler_params=pltpu.CompilerParams(
            collective_id=0, has_side_effects=True, vmem_limit_bytes=40 * 1024 * 1024
        ),
    )(
        residuals[:, 0, 0, 0],
        weights[0, 0, 0],
        fraction[0, 0, 0],
        voxels[:, 0, 0, 0],
        kernel_reach[None, :],
    )
    return jnp.transpose(maps + carry[:, :, None], (0, 2, 1, 3))


def solution(mesh):
    placed = (
        P(None, "tf", "gz", "sec", None, None),
        P("tf", "gz", "sec", None, None),
        P("tf", "gz", "sec", None, None),
        P(None, "tf", "gz", "sec", None, None),
        P("sec"),
    )
    return jax.shard_map(
        per_device,
        mesh=mesh,
        in_specs=placed,
        out_specs=P(None, ("tf", "gz"), "sec", None),
        check_vma=False,
    )
```
